32 devices in a mesh: seq: 8 (over z, x), head: 4 (over y, core).
Axes of the slice: x: 2, y: 2, z: 4, core: 2. Of those that a mesh axis runs over, the one named last changes fastest.
Arguments:
- features: bfloat16 [1024, 4096], P('seq', 'head'), may hold values from -6 to 6
- proj_weight: bfloat16 [4096, 4096], P(None, 'head'), may hold values from -0.09375 to 0.09375
- query_vectors: bfloat16 [1024, 4096], P('seq', 'head'), may hold values from -6 to 6
- key_vectors: bfloat16 [1024, 4096], P('seq', 'head'), may hold values from -6 to 6
Outputs:
- rotated_queries: bfloat16 [1024, 4096], P('seq', 'head')
- rotated_keys: bfloat16 [1024, 4096], P('seq', 'head')
The draws below stay inside these ranges and needn't reach their ends.
All inputs are finite; a program needn't handle non-finite values.
Results may differ from the reference program's by a relative error of at most 0.0024.
Values may be sent and summed in bfloat16 or wider, within the bound.
A program may use at most 128 MiB of HBM per device.

```python
import jax
import jax.numpy as jnp
from jax import lax

D = 4096
HEADS = 32
HEAD_DIM = 128
TOKENS = 1024


def levels(rng, dims, shards, smallest, high):
    def one(position, parts):
        heights = jax.random.uniform(jax.random.fold_in(jax.random.fold_in(rng, 6), position), (parts,), jnp.float32, smallest / len(shards), high / len(shards))
        return jnp.repeat(jnp.exp(heights), dims[position] // parts).reshape((-1,) + (1,) * (len(dims) - position - 1))

    loudness = one(*shards[0])
    for cut in shards[1:]:
        loudness = loudness * one(*cut)
    return loudness


def centred(stream_key, extent, scale, most, cuts=(), kind=jnp.bfloat16):
    values = scale * jax.random.normal(stream_key, extent, jnp.float32)
    if cuts:
        values = values * levels(stream_key, extent, cuts, -0.22, 0.18)
    return jnp.clip(values, -most, most).astype(kind)


def setup_inputs(seed: int = 0) -> dict:
    keys = jax.random.split(jax.random.key(seed), 5)
    return {
        "features": centred(keys[0], (TOKENS, D), 1.0, 6.0, ((0, 8), (1, 4))),
        "proj_weight": centred(keys[1], (D, HEADS * HEAD_DIM), D ** -0.5, 0.09375, ((1, 4),)),
        "query_vectors": centred(keys[2], (TOKENS, HEADS * HEAD_DIM), 1.0, 6.0, ((0, 8), (1, 4))),
        "key_vectors": centred(keys[3], (TOKENS, HEADS * HEAD_DIM), 1.0, 6.0, ((0, 8), (1, 4))),
    }


def reference(features, proj_weight, query_vectors, key_vectors):
    highest = lax.Precision.HIGHEST
    raw_proj = jnp.dot(features, proj_weight, preferred_element_type=jnp.float32)
    raw_proj = raw_proj.reshape(TOKENS, HEADS, HEAD_DIM)
    directions = raw_proj * lax.rsqrt(lax.optimization_barrier(jnp.sum(raw_proj * raw_proj, axis=-1, keepdims=True)) + 1e-06)
    queries = query_vectors.astype(jnp.float32).reshape(TOKENS, HEADS, HEAD_DIM)
    keys_all = key_vectors.astype(jnp.float32).reshape(TOKENS, HEADS, HEAD_DIM)

    def advance(product, item):
        vector, query_row, key_row = item
        along = jnp.einsum('hde,he->hd', product, vector, precision=highest)
        product = product - 2.0 * along[:, :, None] * vector[:, None, :]
        out_query = jnp.einsum('hde,he->hd', product, query_row, precision=highest)
        out_key = jnp.einsum('hde,he->hd', product, key_row, precision=highest)
        return (product, (out_query, out_key))
    start = jnp.broadcast_to(jnp.eye(HEAD_DIM, dtype=jnp.float32), (HEADS, HEAD_DIM, HEAD_DIM))
    final, outputs = lax.scan(advance, start, (directions, queries, keys_all))
    rotated_queries = outputs[0].reshape(TOKENS, HEADS * HEAD_DIM).astype(jnp.bfloat16)
    rotated_keys = outputs[1].reshape(TOKENS, HEADS * HEAD_DIM).astype(jnp.bfloat16)
    return (rotated_queries, rotated_keys)
```

```python
import functools

import jax
import jax.numpy as jnp
from jax import lax
from jax.experimental import pallas as pl
from jax.experimental.pallas import tpu as pltpu
from jax.sharding import PartitionSpec as P

HEAD_DIM = 128
CHUNKS = 2
MESH = pl.DeviceIdType.MESH
F32 = jnp.float32
BF16 = jnp.bfloat16


def split(x):
    hi = x.astype(BF16)
    return hi, (x - hi.astype(F32)).astype(BF16)


def left_of(x):
    return jnp.concatenate(split(x), axis=1)


def right_of(x):
    row = jnp.concatenate(split(x), axis=1)
    return jnp.concatenate([row, row], axis=0)


def fold(r):
    half = r.shape[1] // 2
    return r[:, :half] + r[:, half:]


def product(left, right):
    return fold(jnp.dot(left, right, preferred_element_type=F32))


def product_t(left, right):
    return fold(lax.dot_general(left, right, (((1,), (1,)), ((), ())), preferred_element_type=F32))


def mm(a, b):
    return product(left_of(a), right_of(b))


def kernel(
    n_seq, feat_ref, w_hbm, q_ref, k_ref, oq_ref, ok_ref,
    w_buf, near, far, across, acc, w_dir, v_buf, local, pair, ct, chain, toward, other, outgoing,
    w_sem, gs_sem, gr_sem, s_sem, r_sem,
):
    seq, head = lax.axis_index("seq"), lax.axis_index("head")
    n_pairs = n_seq // 2
    x = seq % 2
    z = seq // 2
    partner = seq + 1 - 2 * x
    sibling = head + 1 - 2 * (head % 2)
    opposite = (head + 2) % 4
    diagonal = (sibling + 2) % 4
    tok, depth = feat_ref.shape
    heads = acc.shape[0]
    half = heads // 2
    piece = depth // CHUNKS
    dim = HEAD_DIM

    loads = []
    for j, owner in enumerate((head, sibling, opposite, diagonal)):
        load = pltpu.make_async_copy(
            w_hbm.at[pl.ds(pl.multiple_of(owner * depth, depth), depth), :], w_buf.at[j], w_sem.at[j]
        )
        load.start()
        loads.append(load)

    barrier = pltpu.get_barrier_semaphore()
    for target in ({"seq": partner}, {"head": sibling}, {"head": opposite}):
        pl.semaphore_signal(barrier, inc=1, device_id=target, device_id_type=MESH)

    @pl.when(z < n_pairs - 1)
    def _():
        pl.semaphore_signal(barrier, inc=1, device_id={"seq": seq + 2}, device_id_type=MESH)

    @pl.when(z > 0)
    def _():
        pl.semaphore_signal(barrier, inc=1, device_id={"seq": seq - 2}, device_id_type=MESH)

    both = jnp.where(z > 0, 1, 0) + jnp.where(z < n_pairs - 1, 1, 0)
    pl.semaphore_wait(barrier, 3 + both)

    def remote(src, dst, send, recv, target):
        return pltpu.make_async_remote_copy(
            src_ref=src, dst_ref=dst, send_sem=send, recv_sem=recv, device_id=target, device_id_type=MESH
        )

    to_far = []
    for c in range(CHUNKS):
        copy = remote(
            feat_ref.at[:, c * piece:(c + 1) * piece], far.at[c], gs_sem.at[1 + c], gr_sem.at[1 + c], {"head": opposite}
        )
        copy.start()
        to_far.append(copy)
    to_near = remote(feat_ref, near, gs_sem.at[0], gr_sem.at[0], {"head": sibling})
    to_near.start()

    def project(block, rows, first=False):
        for n in range(heads // 2):
            columns = slice(n * 2 * dim, (n + 1) * 2 * dim)
            part = jnp.dot(block, rows[:, columns], preferred_element_type=F32)
            for m in range(2):
                value = part[:, m * dim:(m + 1) * dim]
                if first:
                    acc[2 * n + m] = value
                else:
                    acc[2 * n + m] += value

    loads[0].wait()
    project(feat_ref[...], w_buf.at[0], True)
    loads[1].wait()
    to_near.wait_recv()
    project(near[...], w_buf.at[1])
    loads[2].wait()
    loads[3].wait()
    to_across = []
    for c in range(CHUNKS):
        to_far[c].wait_recv()
        copy = remote(far.at[c], across.at[c], gs_sem.at[1 + CHUNKS + c], gr_sem.at[1 + CHUNKS + c], {"head": sibling})
        copy.start()
        to_across.append(copy)
        rows = pl.ds(c * piece, piece)
        project(far[c], w_buf.at[2, rows])
        copy.wait_recv()
        project(across[c], w_buf.at[3, rows])

    i_pos = lax.broadcasted_iota(jnp.int32, (tok, tok), 0)
    j_pos = lax.broadcasted_iota(jnp.int32, (tok, tok), 1)
    eye = jnp.where(i_pos == j_pos, 1.0, 0.0).astype(F32)

    def group(g, at_end):
        ws, grams, inverses = [], [], []
        for i in range(half):
            raw = acc[g * half + i]
            w = raw * lax.rsqrt(jnp.sum(raw * raw, axis=-1, keepdims=True) + 1e-06)
            w_dir[g * half + i] = w
            ws.append(w)
        for w in ws:
            hi, lo = split(w)
            right = jnp.concatenate(
                [jnp.concatenate([hi, hi], axis=1), jnp.concatenate([lo, lo], axis=1)], axis=0
            )
            grams.append(product_t(jnp.concatenate([hi, lo], axis=1), right))
        size = 1
        while size < tok:
            mask = (i_pos // (2 * size) == j_pos // (2 * size)) & (i_pos // size > j_pos // size)
            if size == 1:
                inverses = [2.0 * eye - 4.0 * jnp.where(mask, gram, 0.0) for gram in grams]
            else:
                rights = [right_of(inv) for inv in inverses]
                middles = [
                    product(left_of(jnp.where(mask, gram, 0.0)), right) for gram, right in zip(grams, rights)
                ]
                inverses = [inv - mm(inv, middle) for inv, middle in zip(inverses, middles)]
            size *= 2
        vs = [mm(inv, w) for inv, w in zip(inverses, ws)]
        for i in range(half):
            v_buf[g * half + i] = vs[i]
            at_end(i, eye - mm(ws[i].T, vs[i]))

    first = []
    for i in range(half):
        first.append(remote(outgoing.at[i], pair.at[x, i], s_sem.at[0, i], r_sem.at[0, i], {"seq": partner}))

    def send_off(i, value):
        outgoing[i] = value
        first[i].start()

    def keep(i, value):
        pair[x, i] = value

    group(1 - x, send_off)
    group(x, keep)

    below = lax.broadcasted_iota(jnp.int32, (2 * tok, tok), 0) % tok >= lax.broadcasted_iota(jnp.int32, (2 * tok, tok), 1)
    for hh in range(heads):
        columns = slice(hh * dim, (hh + 1) * dim)
        targets = jnp.concatenate([q_ref[:, columns], k_ref[:, columns]], axis=0)
        along = product_t(targets, jnp.concatenate(split(w_dir[hh]), axis=0))
        local[hh] = left_of(targets.astype(F32) - mm(jnp.where(below, along, 0.0), v_buf[hh]))

    chained, last = [], []
    for i in range(half):
        chained.append(remote(ct.at[i], chain.at[i], s_sem.at[1, i], r_sem.at[1, i], {"seq": seq + 2}))
        last.append(remote(toward.at[i], other.at[i], s_sem.at[2, i], r_sem.at[2, i], {"seq": partner}))

    @pl.when(z == 0)
    def _():
        for i in range(half):
            chain[i] = eye

    for i in range(half):
        pltpu.make_async_remote_copy(
            src_ref=outgoing.at[i], dst_ref=pair.at[1 - x, i], send_sem=s_sem.at[0, i], recv_sem=r_sem.at[0, i],
            device_id={"seq": partner}, device_id_type=MESH,
        ).wait_recv()
        ct[i] = mm(pair[1, i], pair[0, i])

    for i in range(half):
        @pl.when(z > 0)
        def _():
            chained[i].wait_recv()

            @pl.when(z < n_pairs - 1)
            def _():
                ct[i] = mm(ct[i], chain[i])

        @pl.when(z < n_pairs - 1)
        def _():
            chained[i].start()

        even = chain[i]
        odd = mm(pair[0, i], even)
        toward[i] = jnp.where(x == 0, odd, even)
        last[i].start()
        mine = jnp.where(x == 0, even, odd)
        finish(x * half + i, mine, local, oq_ref, ok_ref)

    for i in range(half):
        last[i].wait_recv()
        finish((1 - x) * half + i, other[i], local, oq_ref, ok_ref)

    to_near.wait_send()
    for c in range(CHUNKS):
        to_far[c].wait_send()
        to_across[c].wait_send()
    for i in range(half):
        first[i].wait_send()
        last[i].wait_send()

    @pl.when(z < n_pairs - 1)
    def _():
        for i in range(half):
            chained[i].wait_send()


def finish(hh, entering, local, oq_ref, ok_ref):
    tok = oq_ref.shape[0]
    out = product(local[hh], right_of(entering)).astype(BF16)
    columns = pl.ds(pl.multiple_of(hh * HEAD_DIM, HEAD_DIM), HEAD_DIM)
    oq_ref[:, columns] = out[:tok]
    ok_ref[:, columns] = out[tok:]


def solution(mesh):
    n_seq = mesh.shape["seq"]

    def body(features, proj_weight, query_vectors, key_vectors):
        tok, depth = features.shape
        width = proj_weight.shape[1]
        heads = width // HEAD_DIM
        half = heads // 2
        square = (HEAD_DIM, HEAD_DIM)
        vmem = pl.BlockSpec(memory_space=pltpu.VMEM)
        out = jax.ShapeDtypeStruct((tok, width), BF16)
        return pl.pallas_call(
            functools.partial(kernel, n_seq),
            out_shape=(out, out),
            in_specs=[vmem, pl.BlockSpec(memory_space=pl.ANY), vmem, vmem],
            out_specs=(vmem, vmem),
            scratch_shapes=[
                pltpu.VMEM((4, depth, width), BF16),
                pltpu.VMEM((tok, depth), BF16),
                pltpu.VMEM((CHUNKS, tok, depth // CHUNKS), BF16),
                pltpu.VMEM((CHUNKS, tok, depth // CHUNKS), BF16),
                pltpu.VMEM((heads, tok, HEAD_DIM), F32),
                pltpu.VMEM((heads, tok, HEAD_DIM), F32),
                pltpu.VMEM((heads, tok, HEAD_DIM), F32),
                pltpu.VMEM((heads, 2 * tok, 2 * HEAD_DIM), BF16),
                pltpu.VMEM((2, half) + square, F32),
                pltpu.VMEM((half,) + square, F32),
                pltpu.VMEM((half,) + square, F32),
                pltpu.VMEM((half,) + square, F32),
                pltpu.VMEM((half,) + square, F32),
                pltpu.VMEM((half,) + square, F32),
                pltpu.SemaphoreType.DMA((4,)),
                pltpu.SemaphoreType.DMA((1 + 2 * CHUNKS,)),
                pltpu.SemaphoreType.DMA((1 + 2 * CHUNKS,)),
                pltpu.SemaphoreType.DMA((3, half)),
                pltpu.SemaphoreType.DMA((3, half)),
            ],
            compiler_params=pltpu.CompilerParams(
                collective_id=0, has_side_effects=True, vmem_limit_bytes=56 * 1024 * 1024
            ),
            cost_estimate=pl.CostEstimate(flops=4_000_000_000, bytes_accessed=10_000_000, transcendentals=0),
        )(features, proj_weight, query_vectors, key_vectors)

    in_specs = (P("seq", "head"), P(None, "head"), P("seq", "head"), P("seq", "head"))
    out_specs = (P("seq", "head"), P("seq", "head"))
    return jax.shard_map(body, mesh=mesh, in_specs=in_specs, out_specs=out_specs, check_vma=False)
```

```python
import functools

import jax
import jax.numpy as jnp
from jax import lax
from jax.experimental import pallas as pl
from jax.experimental.pallas import tpu as pltpu
from jax.sharding import PartitionSpec as P

HEAD_DIM = 128
CHUNKS = 2
MESH = pl.DeviceIdType.MESH
F32 = jnp.float32
BF16 = jnp.bfloat16


def split(x):
    hi = x.astype(BF16)
    return hi, (x - hi.astype(F32)).astype(BF16)


def left_of(x):
    return jnp.concatenate(split(x), axis=1)


def right_of(x):
    row = jnp.concatenate(split(x), axis=1)
    return jnp.concatenate([row, row], axis=0)


def fold(r):
    half = r.shape[1] // 2
    return r[:, :half] + r[:, half:]


def product(left, right):
    return fold(jnp.dot(left, right, preferred_element_type=F32))


def product_t(left, right):
    return fold(lax.dot_general(left, right, (((1,), (1,)), ((), ())), preferred_element_type=F32))


def mm(a, b):
    return product(left_of(a), right_of(b))


def kernel(
    n_seq, feat_hbm, w_hbm, q_hbm, k_hbm, out_ref,
    feat_ref, x_ref, w_buf, near, far, across, acc, w_dir, v_buf, local, pair, ct, chain, toward, other, outgoing,
    w_sem, gs_sem, gr_sem, s_sem, r_sem,
):
    seq, head = lax.axis_index("seq"), lax.axis_index("head")
    n_pairs = n_seq // 2
    x = seq % 2
    z = seq // 2
    partner = seq + 1 - 2 * x
    sibling = head + 1 - 2 * (head % 2)
    opposite = (head + 2) % 4
    diagonal = (sibling + 2) % 4
    tok, depth = feat_hbm.shape
    heads = acc.shape[0]
    half = heads // 2
    piece = depth // CHUNKS
    dim = HEAD_DIM

    feat_load = pltpu.make_async_copy(feat_hbm, feat_ref, w_sem.at[4])
    feat_load.start()
    loads = []
    for j, owner in enumerate((head, sibling, opposite, diagonal)):
        load = pltpu.make_async_copy(
            w_hbm.at[pl.ds(pl.multiple_of(owner * depth, depth), depth), :], w_buf.at[j], w_sem.at[j]
        )
        load.start()
        loads.append(load)
    q_load = pltpu.make_async_copy(q_hbm, x_ref.at[:tok], w_sem.at[5])
    k_load = pltpu.make_async_copy(k_hbm, x_ref.at[tok:], w_sem.at[6])
    q_load.start()
    k_load.start()

    barrier = pltpu.get_barrier_semaphore()
    for target in ({"seq": partner}, {"head": sibling}, {"head": opposite}):
        pl.semaphore_signal(barrier, inc=1, device_id=target, device_id_type=MESH)

    @pl.when(z < n_pairs - 1)
    def _():
        pl.semaphore_signal(barrier, inc=1, device_id={"seq": seq + 2}, device_id_type=MESH)

    @pl.when(z > 0)
    def _():
        pl.semaphore_signal(barrier, inc=1, device_id={"seq": seq - 2}, device_id_type=MESH)

    both = jnp.where(z > 0, 1, 0) + jnp.where(z < n_pairs - 1, 1, 0)
    pl.semaphore_wait(barrier, 3 + both)

    def remote(src, dst, send, recv, target):
        return pltpu.make_async_remote_copy(
            src_ref=src, dst_ref=dst, send_sem=send, recv_sem=recv, device_id=target, device_id_type=MESH
        )

    to_far = []
    for c in range(CHUNKS):
        copy = remote(
            feat_hbm.at[:, c * piece:(c + 1) * piece], far.at[c], gs_sem.at[1 + c], gr_sem.at[1 + c], {"head": opposite}
        )
        copy.start()
        to_far.append(copy)
    to_near = remote(feat_hbm, near, gs_sem.at[0], gr_sem.at[0], {"head": sibling})
    to_near.start()

    def project(block, rows, first=False):
        for n in range(heads // 2):
            columns = slice(n * 2 * dim, (n + 1) * 2 * dim)
            part = jnp.dot(block, rows[:, columns], preferred_element_type=F32)
            for m in range(2):
                value = part[:, m * dim:(m + 1) * dim]
                if first:
                    acc[2 * n + m] = value
                else:
                    acc[2 * n + m] += value

    feat_load.wait()
    loads[0].wait()
    project(feat_ref[...], w_buf.at[0], True)
    loads[1].wait()
    to_near.wait_recv()
    project(near[...], w_buf.at[1])
    loads[2].wait()
    loads[3].wait()
    to_across = []
    for c in range(CHUNKS):
        to_far[c].wait_recv()
        copy = remote(far.at[c], across.at[c], gs_sem.at[1 + CHUNKS + c], gr_sem.at[1 + CHUNKS + c], {"head": sibling})
        copy.start()
        to_across.append(copy)
        rows = pl.ds(c * piece, piece)
        project(far[c], w_buf.at[2, rows])
        copy.wait_recv()
        project(across[c], w_buf.at[3, rows])

    i_pos = lax.broadcasted_iota(jnp.int32, (tok, tok), 0)
    j_pos = lax.broadcasted_iota(jnp.int32, (tok, tok), 1)
    eye = jnp.where(i_pos == j_pos, 1.0, 0.0).astype(F32)

    def group(start, count, at_end):
        ws, grams, inverses = [], [], []
        for i in range(count):
            raw = acc[start + i]
            w = raw * lax.rsqrt(jnp.sum(raw * raw, axis=-1, keepdims=True) + 1e-06)
            w_dir[start + i] = w
            ws.append(w)
        for w in ws:
            hi, lo = split(w)
            right = jnp.concatenate(
                [jnp.concatenate([hi, hi], axis=1), jnp.concatenate([lo, lo], axis=1)], axis=0
            )
            grams.append(product_t(jnp.concatenate([hi, lo], axis=1), right))
        size = 1
        while size < tok:
            mask = (i_pos // (2 * size) == j_pos // (2 * size)) & (i_pos // size > j_pos // size)
            if size == 1:
                inverses = [2.0 * eye - 4.0 * jnp.where(mask, gram, 0.0) for gram in grams]
            else:
                rights = [right_of(inv) for inv in inverses]
                middles = [
                    product(left_of(jnp.where(mask, gram, 0.0)), right) for gram, right in zip(grams, rights)
                ]
                inverses = [inv - mm(inv, middle) for inv, middle in zip(inverses, middles)]
            size *= 2
        vs = [mm(inv, w) for inv, w in zip(inverses, ws)]
        for i in range(count):
            v_buf[start + i] = vs[i]
            at_end(i, eye - mm(ws[i].T, vs[i]))

    first = []
    for i in range(half):
        first.append(remote(outgoing.at[i], pair.at[x, i], s_sem.at[0, i], r_sem.at[0, i], {"seq": partner}))

    def send_off(i, value):
        outgoing[i] = value
        first[i].start()

    def keep(i, value):
        pair[x, i] = value

    def done(i, value):
        @pl.when((i // half) == x)
        def _():
            pair[x, i % half] = value
        @pl.when((i // half) != x)
        def _():
            outgoing[i % half] = value
            first[i % half].start()
    group(0, heads, done)

    q_load.wait()
    k_load.wait()
    below = lax.broadcasted_iota(jnp.int32, (2 * tok, tok), 0) % tok >= lax.broadcasted_iota(jnp.int32, (2 * tok, tok), 1)
    for hh in range(heads):
        columns = slice(hh * dim, (hh + 1) * dim)
        targets = x_ref[:, columns]
        along = product_t(targets, jnp.concatenate(split(w_dir[hh]), axis=0))
        local[hh] = left_of(targets.astype(F32) - mm(jnp.where(below, along, 0.0), v_buf[hh]))

    chained, last = [], []
    for i in range(half):
        chained.append(remote(ct.at[i], chain.at[i], s_sem.at[1, i], r_sem.at[1, i], {"seq": seq + 2}))
        last.append(remote(toward.at[i], other.at[i], s_sem.at[2, i], r_sem.at[2, i], {"seq": partner}))

    @pl.when(z == 0)
    def _():
        for i in range(half):
            chain[i] = eye

    for i in range(half):
        remote(outgoing.at[i], pair.at[1 - x, i], s_sem.at[0, i], r_sem.at[0, i], {"seq": partner}).wait_recv()
        ct[i] = mm(pair[1, i], pair[0, i])

        @pl.when(z > 0)
        def _():
            chained[i].wait_recv()

            @pl.when(z < n_pairs - 1)
            def _():
                ct[i] = mm(ct[i], chain[i])

        @pl.when(z < n_pairs - 1)
        def _():
            chained[i].start()

        @pl.when(x == 0)
        def _():
            toward[i] = mm(pair[0, i], chain[i])

        @pl.when(x == 1)
        def _():
            toward[i] = chain[i]
            chain[i] = mm(pair[0, i], chain[i])

        last[i].start()

    for i in range(half):
        finish(x * half + i, chain[i], local, out_ref)
    for i in range(half):
        last[i].wait_recv()
        finish((1 - x) * half + i, other[i], local, out_ref)

    to_near.wait_send()
    for c in range(CHUNKS):
        to_far[c].wait_send()
        to_across[c].wait_send()
    for i in range(half):
        first[i].wait_send()
        last[i].wait_send()

    @pl.when(z < n_pairs - 1)
    def _():
        for i in range(half):
            chained[i].wait_send()


def finish(hh, entering, local, out_ref):
    out = product(local[hh], right_of(entering)).astype(BF16)
    columns = pl.ds(pl.multiple_of(hh * HEAD_DIM, HEAD_DIM), HEAD_DIM)
    out_ref[:, columns] = out


def part(both_ref, q_ref, k_ref):
    tok = q_ref.shape[0]
    q_ref[...] = both_ref[:tok]
    k_ref[...] = both_ref[tok:]


def solution(mesh):
    n_seq = mesh.shape["seq"]

    def body(features, proj_weight, query_vectors, key_vectors):
        tok, depth = features.shape
        width = proj_weight.shape[1]
        heads = width // HEAD_DIM
        half = heads // 2
        square = (HEAD_DIM, HEAD_DIM)
        vmem = pl.BlockSpec(memory_space=pltpu.VMEM)
        out = jax.ShapeDtypeStruct((tok, width), BF16)
        both = pl.pallas_call(
            functools.partial(kernel, n_seq),
            out_shape=jax.ShapeDtypeStruct((2 * tok, width), BF16),
            in_specs=[pl.BlockSpec(memory_space=pl.ANY)] * 4,
            out_specs=vmem,
            scratch_shapes=[
                pltpu.VMEM((tok, depth), BF16),
                pltpu.VMEM((2 * tok, width), BF16),
                pltpu.VMEM((4, depth, width), BF16),
                pltpu.VMEM((tok, depth), BF16),
                pltpu.VMEM((CHUNKS, tok, depth // CHUNKS), BF16),
                pltpu.VMEM((CHUNKS, tok, depth // CHUNKS), BF16),
                pltpu.VMEM((heads, tok, HEAD_DIM), F32),
                pltpu.VMEM((heads, tok, HEAD_DIM), F32),
                pltpu.VMEM((heads, tok, HEAD_DIM), F32),
                pltpu.VMEM((heads, 2 * tok, 2 * HEAD_DIM), BF16),
                pltpu.VMEM((2, half) + square, F32),
                pltpu.VMEM((half,) + square, F32),
                pltpu.VMEM((half,) + square, F32),
                pltpu.VMEM((half,) + square, F32),
                pltpu.VMEM((half,) + square, F32),
                pltpu.VMEM((half,) + square, F32),
                pltpu.SemaphoreType.DMA((7,)),
                pltpu.SemaphoreType.DMA((1 + 2 * CHUNKS,)),
                pltpu.SemaphoreType.DMA((1 + 2 * CHUNKS,)),
                pltpu.SemaphoreType.DMA((3, half)),
                pltpu.SemaphoreType.DMA((3, half)),
            ],
            compiler_params=pltpu.CompilerParams(
                collective_id=0, has_side_effects=True, vmem_limit_bytes=56 * 1024 * 1024
            ),
            cost_estimate=pl.CostEstimate(flops=4_000_000_000, bytes_accessed=10_000_000, transcendentals=0),
        )(features, proj_weight, query_vectors, key_vectors)
        return pl.pallas_call(part, out_shape=(out, out), in_specs=[vmem], out_specs=(vmem, vmem))(both)

    in_specs = (P("seq", "head"), P(None, "head"), P("seq", "head"), P("seq", "head"))
    out_specs = (P("seq", "head"), P("seq", "head"))
    return jax.shard_map(body, mesh=mesh, in_specs=in_specs, out_specs=out_specs, check_vma=False)
```

```python
import functools

import jax
import jax.numpy as jnp
from jax import lax
from jax.experimental import pallas as pl
from jax.experimental.pallas import tpu as pltpu
from jax.sharding import PartitionSpec as P

HEAD_DIM = 128
CHUNKS = 2
CUTS = 2
MESH = pl.DeviceIdType.MESH
F32 = jnp.float32
BF16 = jnp.bfloat16


def split(x):
    hi = x.astype(BF16)
    return hi, (x - hi.astype(F32)).astype(BF16)


def left_of(x):
    return jnp.concatenate(split(x), axis=1)


def right_of(x):
    row = jnp.concatenate(split(x), axis=1)
    return jnp.concatenate([row, row], axis=0)


def fold(r):
    half = r.shape[1] // 2
    return r[:, :half] + r[:, half:]


def product(left, right):
    return fold(jnp.dot(left, right, preferred_element_type=F32))


def product_t(left, right):
    return fold(lax.dot_general(left, right, (((1,), (1,)), ((), ())), preferred_element_type=F32))


def mm(a, b):
    return product(left_of(a), right_of(b))


def kernel(
    n_seq, feat_hbm, w_hbm, q_hbm, k_hbm, out_ref,
    feat_ref, x_ref, w_buf, near, far, across, acc, w_dir, v_buf, local, pair, ct, chain, toward, other, outgoing, mine,
    w_sem, gs_sem, gr_sem, s_sem, r_sem,
):
    seq, head = lax.axis_index("seq"), lax.axis_index("head")
    n_pairs = n_seq // 2
    x = seq % 2
    z = seq // 2
    partner = seq + 1 - 2 * x
    sibling = head + 1 - 2 * (head % 2)
    opposite = (head + 2) % 4
    diagonal = (sibling + 2) % 4
    tok, depth = feat_hbm.shape
    heads = acc.shape[0]
    half = heads // 2
    piece = depth // CHUNKS
    dim = HEAD_DIM

    feat_load = pltpu.make_async_copy(feat_hbm, feat_ref, w_sem.at[4])
    feat_load.start()
    loads = []
    for j, owner in enumerate((head, sibling, opposite, diagonal)):
        load = pltpu.make_async_copy(
            w_hbm.at[pl.ds(pl.multiple_of(owner * depth, depth), depth), :], w_buf.at[j], w_sem.at[j]
        )
        load.start()
        loads.append(load)
    q_load = pltpu.make_async_copy(q_hbm, x_ref.at[:tok], w_sem.at[5])
    k_load = pltpu.make_async_copy(k_hbm, x_ref.at[tok:], w_sem.at[6])
    q_load.start()
    k_load.start()

    barrier = pltpu.get_barrier_semaphore()
    for target in ({"seq": partner}, {"head": sibling}, {"head": opposite}):
        pl.semaphore_signal(barrier, inc=1, device_id=target, device_id_type=MESH)

    @pl.when(z < n_pairs - 1)
    def _():
        pl.semaphore_signal(barrier, inc=1, device_id={"seq": seq + 2}, device_id_type=MESH)

    @pl.when(z > 0)
    def _():
        pl.semaphore_signal(barrier, inc=1, device_id={"seq": seq - 2}, device_id_type=MESH)

    both = jnp.where(z > 0, 1, 0) + jnp.where(z < n_pairs - 1, 1, 0)
    pl.semaphore_wait(barrier, 3 + both)

    def remote(src, dst, send, recv, target):
        return pltpu.make_async_remote_copy(
            src_ref=src, dst_ref=dst, send_sem=send, recv_sem=recv, device_id=target, device_id_type=MESH
        )

    to_far = []
    for c in range(CHUNKS):
        copy = remote(
            feat_hbm.at[:, c * piece:(c + 1) * piece], far.at[c], gs_sem.at[1 + c], gr_sem.at[1 + c], {"head": opposite}
        )
        copy.start()
        to_far.append(copy)
    to_near = remote(feat_hbm, near, gs_sem.at[0], gr_sem.at[0], {"head": sibling})
    to_near.start()

    def project(block, rows, first=False):
        for n in range(heads // 2):
            columns = slice(n * 2 * dim, (n + 1) * 2 * dim)
            part = jnp.dot(block, rows[:, columns], preferred_element_type=F32)
            for m in range(2):
                value = part[:, m * dim:(m + 1) * dim]
                if first:
                    acc[2 * n + m] = value
                else:
                    acc[2 * n + m] += value

    feat_load.wait()
    loads[0].wait()
    project(feat_ref[...], w_buf.at[0], True)
    loads[1].wait()
    to_near.wait_recv()
    project(near[...], w_buf.at[1])
    loads[2].wait()
    loads[3].wait()
    to_across = []
    for c in range(CHUNKS):
        to_far[c].wait_recv()
        copy = remote(far.at[c], across.at[c], gs_sem.at[1 + CHUNKS + c], gr_sem.at[1 + CHUNKS + c], {"head": sibling})
        copy.start()
        to_across.append(copy)
        rows = pl.ds(c * piece, piece)
        project(far[c], w_buf.at[2, rows])
        copy.wait_recv()
        project(across[c], w_buf.at[3, rows])

    i_pos = lax.broadcasted_iota(jnp.int32, (tok, tok), 0)
    j_pos = lax.broadcasted_iota(jnp.int32, (tok, tok), 1)
    eye = jnp.where(i_pos == j_pos, 1.0, 0.0).astype(F32)

    def group(start, count, at_end):
        ws, grams, inverses = [], [], []
        for i in range(count):
            raw = acc[start + i]
            w = raw * lax.rsqrt(jnp.sum(raw * raw, axis=-1, keepdims=True) + 1e-06)
            w_dir[start + i] = w
            ws.append(w)
        for w in ws:
            hi, lo = split(w)
            right = jnp.concatenate(
                [jnp.concatenate([hi, hi], axis=1), jnp.concatenate([lo, lo], axis=1)], axis=0
            )
            grams.append(product_t(jnp.concatenate([hi, lo], axis=1), right))
        size = 1
        while size < tok:
            mask = (i_pos // (2 * size) == j_pos // (2 * size)) & (i_pos // size > j_pos // size)
            if size == 1:
                inverses = [2.0 * eye - 4.0 * jnp.where(mask, gram, 0.0) for gram in grams]
            else:
                rights = [right_of(inv) for inv in inverses]
                middles = [
                    product(left_of(jnp.where(mask, gram, 0.0)), right) for gram, right in zip(grams, rights)
                ]
                inverses = [inv - mm(inv, middle) for inv, middle in zip(inverses, middles)]
            size *= 2
        vs = [mm(inv, w) for inv, w in zip(inverses, ws)]
        for i in range(count):
            v_buf[start + i] = vs[i]
            at_end(i, eye - mm(vs[i].T, ws[i]))

    first = []
    for i in range(half):
        first.append(remote(outgoing.at[i], pair.at[x, i], s_sem.at[0, i], r_sem.at[0, i], {"seq": partner}))

    def send_off(i, value):
        outgoing[i] = value
        first[i].start()

    def keep(i, value):
        pair[x, i] = value

    def done(i, value):
        @pl.when((i // half) == x)
        def _():
            pair[x, i % half] = value
        @pl.when((i // half) != x)
        def _():
            outgoing[i % half] = value
            first[i % half].start()
    group(0, heads, done)

    q_load.wait()
    k_load.wait()
    below = lax.broadcasted_iota(jnp.int32, (2 * tok, tok), 0) % tok >= lax.broadcasted_iota(jnp.int32, (2 * tok, tok), 1)
    for hh in range(heads):
        columns = slice(hh * dim, (hh + 1) * dim)
        targets = x_ref[:, columns]
        along = product_t(targets, jnp.concatenate(split(w_dir[hh]), axis=0))
        local[hh] = left_of(targets.astype(F32) - mm(jnp.where(below, along, 0.0), v_buf[hh]))

    rows = tok // CUTS
    pieces = [(i, pl.ds(r * rows, rows)) for i in range(half) for r in range(CUTS)]
    chained, last = [], []
    for p, (i, cut) in enumerate(pieces):
        chained.append(remote(ct.at[i, cut], chain.at[i, cut], s_sem.at[1, p], r_sem.at[1, p], {"seq": seq + 2}))
        last.append(remote(toward.at[i, cut], other.at[i, cut], s_sem.at[2, p], r_sem.at[2, p], {"seq": partner}))

    @pl.when(z == 0)
    def _():
        for i in range(half):
            chain[i] = eye

    for i in range(half):
        remote(outgoing.at[i], pair.at[1 - x, i], s_sem.at[0, i], r_sem.at[0, i], {"seq": partner}).wait_recv()
        even = right_of(pair[0, i])
        step = jnp.concatenate([right_of(product(left_of(pair[0, i]), right_of(pair[1, i]))), even], axis=1)
        for r in range(CUTS):
            p = i * CUTS + r
            cut = pieces[p][1]

            @pl.when(z > 0)
            def _():
                chained[p].wait_recv()

            before = chain[i, cut]
            after = jnp.dot(left_of(before), step, preferred_element_type=F32)
            ct[i, cut] = fold(after[:, :2 * dim])

            @pl.when(z < n_pairs - 1)
            def _():
                chained[p].start()

            odd = fold(after[:, 2 * dim:])
            toward[i, cut] = jnp.where(x == 0, odd, before)
            last[p].start()
            mine[i, cut] = jnp.where(x == 0, before, odd)

    for i in range(half):
        finish(x * half + i, mine[i], local, out_ref)
    for i in range(half):
        for r in range(CUTS):
            last[i * CUTS + r].wait_recv()
        finish((1 - x) * half + i, other[i], local, out_ref)

    to_near.wait_send()
    for c in range(CHUNKS):
        to_far[c].wait_send()
        to_across[c].wait_send()
    for i in range(half):
        first[i].wait_send()
    for copy in last:
        copy.wait_send()

    @pl.when(z < n_pairs - 1)
    def _():
        for copy in chained:
            copy.wait_send()


def finish(hh, entering, local, out_ref):
    hi, lo = split(entering)
    both = jnp.concatenate([jnp.concatenate([hi, hi], axis=1), jnp.concatenate([lo, lo], axis=1)], axis=0)
    out = product_t(local[hh], both).astype(BF16)
    columns = pl.ds(pl.multiple_of(hh * HEAD_DIM, HEAD_DIM), HEAD_DIM)
    out_ref[:, columns] = out


def part(both_ref, q_ref, k_ref):
    tok = q_ref.shape[0]
    q_ref[...] = both_ref[:tok]
    k_ref[...] = both_ref[tok:]


def solution(mesh):
    n_seq = mesh.shape["seq"]

    def body(features, proj_weight, query_vectors, key_vectors):
        tok, depth = features.shape
        width = proj_weight.shape[1]
        heads = width // HEAD_DIM
        half = heads // 2
        square = (HEAD_DIM, HEAD_DIM)
        vmem = pl.BlockSpec(memory_space=pltpu.VMEM)
        out = jax.ShapeDtypeStruct((tok, width), BF16)
        both = pl.pallas_call(
            functools.partial(kernel, n_seq),
            out_shape=jax.ShapeDtypeStruct((2 * tok, width), BF16),
            in_specs=[pl.BlockSpec(memory_space=pl.ANY)] * 4,
            out_specs=vmem,
            scratch_shapes=[
                pltpu.VMEM((tok, depth), BF16),
                pltpu.VMEM((2 * tok, width), BF16),
                pltpu.VMEM((4, depth, width), BF16),
                pltpu.VMEM((tok, depth), BF16),
                pltpu.VMEM((CHUNKS, tok, depth // CHUNKS), BF16),
                pltpu.VMEM((CHUNKS, tok, depth // CHUNKS), BF16),
                pltpu.VMEM((heads, tok, HEAD_DIM), F32),
                pltpu.VMEM((heads, tok, HEAD_DIM), F32),
                pltpu.VMEM((heads, tok, HEAD_DIM), F32),
                pltpu.VMEM((heads, 2 * tok, 2 * HEAD_DIM), BF16),
                pltpu.VMEM((2, half) + square, F32),
                pltpu.VMEM((half,) + square, F32),
                pltpu.VMEM((half,) + square, F32),
                pltpu.VMEM((half,) + square, F32),
                pltpu.VMEM((half,) + square, F32),
                pltpu.VMEM((half,) + square, F32),
                pltpu.VMEM((half,) + square, F32),
                pltpu.SemaphoreType.DMA((7,)),
                pltpu.SemaphoreType.DMA((1 + 2 * CHUNKS,)),
                pltpu.SemaphoreType.DMA((1 + 2 * CHUNKS,)),
                pltpu.SemaphoreType.DMA((3, half * CUTS)),
                pltpu.SemaphoreType.DMA((3, half * CUTS)),
            ],
            compiler_params=pltpu.CompilerParams(
                collective_id=0, has_side_effects=True, vmem_limit_bytes=56 * 1024 * 1024
            ),
            cost_estimate=pl.CostEstimate(flops=4_000_000_000, bytes_accessed=10_000_000, transcendentals=0),
        )(features, proj_weight, query_vectors, key_vectors)
        return pl.pallas_call(part, out_shape=(out, out), in_specs=[vmem], out_specs=(vmem, vmem))(both)

    in_specs = (P("seq", "head"), P(None, "head"), P("seq", "head"), P("seq", "head"))
    out_specs = (P("seq", "head"), P("seq", "head"))
    return jax.shard_map(body, mesh=mesh, in_specs=in_specs, out_specs=out_specs, check_vma=False)
```

```python
import functools

import jax
import jax.numpy as jnp
from jax import lax
from jax.experimental import pallas as pl
from jax.experimental.pallas import tpu as pltpu
from jax.sharding import PartitionSpec as P

HEAD_DIM = 128
CHUNKS = 2
CUTS = 4
MESH = pl.DeviceIdType.MESH
F32 = jnp.float32
BF16 = jnp.bfloat16


def split(x):
    hi = x.astype(BF16)
    return hi, (x - hi.astype(F32)).astype(BF16)


def left_of(x):
    return jnp.concatenate(split(x), axis=1)


def right_of(x):
    row = jnp.concatenate(split(x), axis=1)
    return jnp.concatenate([row, row], axis=0)


def fold(r):
    half = r.shape[1] // 2
    return r[:, :half] + r[:, half:]


def product(left, right):
    return fold(jnp.dot(left, right, preferred_element_type=F32))


def product_t(left, right):
    return fold(lax.dot_general(left, right, (((1,), (1,)), ((), ())), preferred_element_type=F32))


def mm(a, b):
    return product(left_of(a), right_of(b))


def kernel(
    n_seq, feat_hbm, w_hbm, q_hbm, k_hbm, out_ref,
    feat_ref, x_ref, w_buf, near, far, across, acc, w_dir, v_buf, local, pair, ct, chain, toward, other, outgoing, mine,
    w_sem, gs_sem, gr_sem, s_sem, r_sem,
):
    seq, head = lax.axis_index("seq"), lax.axis_index("head")
    n_pairs = n_seq // 2
    x = seq % 2
    z = seq // 2
    partner = seq + 1 - 2 * x
    sibling = head + 1 - 2 * (head % 2)
    opposite = (head + 2) % 4
    diagonal = (sibling + 2) % 4
    tok, depth = feat_hbm.shape
    heads = acc.shape[0]
    half = heads // 2
    piece = depth // CHUNKS
    dim = HEAD_DIM

    feat_load = pltpu.make_async_copy(feat_hbm, feat_ref, w_sem.at[4])
    feat_load.start()
    loads = []
    for j, owner in enumerate((head, sibling, opposite, diagonal)):
        load = pltpu.make_async_copy(
            w_hbm.at[pl.ds(pl.multiple_of(owner * depth, depth), depth), :], w_buf.at[j], w_sem.at[j]
        )
        load.start()
        loads.append(load)
    q_load = pltpu.make_async_copy(q_hbm, x_ref.at[:tok], w_sem.at[5])
    k_load = pltpu.make_async_copy(k_hbm, x_ref.at[tok:], w_sem.at[6])
    q_load.start()
    k_load.start()

    barrier = pltpu.get_barrier_semaphore()
    for target in ({"seq": partner}, {"head": sibling}, {"head": opposite}):
        pl.semaphore_signal(barrier, inc=1, device_id=target, device_id_type=MESH)

    @pl.when(z < n_pairs - 1)
    def _():
        pl.semaphore_signal(barrier, inc=1, device_id={"seq": seq + 2}, device_id_type=MESH)

    @pl.when(z > 0)
    def _():
        pl.semaphore_signal(barrier, inc=1, device_id={"seq": seq - 2}, device_id_type=MESH)

    both = jnp.where(z > 0, 1, 0) + jnp.where(z < n_pairs - 1, 1, 0)
    pl.semaphore_wait(barrier, 3 + both)

    def remote(src, dst, send, recv, target):
        return pltpu.make_async_remote_copy(
            src_ref=src, dst_ref=dst, send_sem=send, recv_sem=recv, device_id=target, device_id_type=MESH
        )

    to_far = []
    for c in range(CHUNKS):
        copy = remote(
            feat_hbm.at[:, c * piece:(c + 1) * piece], far.at[c], gs_sem.at[1 + c], gr_sem.at[1 + c], {"head": opposite}
        )
        copy.start()
        to_far.append(copy)
    to_near = remote(feat_hbm, near, gs_sem.at[0], gr_sem.at[0], {"head": sibling})
    to_near.start()

    def project(block, rows, first=False):
        for n in range(heads // 2):
            columns = slice(n * 2 * dim, (n + 1) * 2 * dim)
            part = jnp.dot(block, rows[:, columns], preferred_element_type=F32)
            for m in range(2):
                value = part[:, m * dim:(m + 1) * dim]
                if first:
                    acc[2 * n + m] = value
                else:
                    acc[2 * n + m] += value

    feat_load.wait()
    loads[0].wait()
    project(feat_ref[...], w_buf.at[0], True)
    loads[1].wait()
    to_near.wait_recv()
    project(near[...], w_buf.at[1])
    loads[2].wait()
    loads[3].wait()
    to_across = []
    for c in range(CHUNKS):
        to_far[c].wait_recv()
        copy = remote(far.at[c], across.at[c], gs_sem.at[1 + CHUNKS + c], gr_sem.at[1 + CHUNKS + c], {"head": sibling})
        copy.start()
        to_across.append(copy)
        rows = pl.ds(c * piece, piece)
        project(far[c], w_buf.at[2, rows])
        copy.wait_recv()
        project(across[c], w_buf.at[3, rows])

    i_pos = lax.broadcasted_iota(jnp.int32, (tok, tok), 0)
    j_pos = lax.broadcasted_iota(jnp.int32, (tok, tok), 1)
    eye = jnp.where(i_pos == j_pos, 1.0, 0.0).astype(F32)

    def group(start, count, at_end):
        ws, grams, inverses = [], [], []
        for i in range(count):
            raw = acc[start + i]
            w = raw * lax.rsqrt(jnp.sum(raw * raw, axis=-1, keepdims=True) + 1e-06)
            w_dir[start + i] = w
            ws.append(w)
        for w in ws:
            hi, lo = split(w)
            right = jnp.concatenate(
                [jnp.concatenate([hi, hi], axis=1), jnp.concatenate([lo, lo], axis=1)], axis=0
            )
            grams.append(product_t(jnp.concatenate([hi, lo], axis=1), right))
        size = 1
        while size < tok:
            mask = (i_pos // (2 * size) == j_pos // (2 * size)) & (i_pos // size > j_pos // size)
            if size == 1:
                inverses = [2.0 * eye - 4.0 * jnp.where(mask, gram, 0.0) for gram in grams]
            else:
                rights = [right_of(inv) for inv in inverses]
                middles = [
                    product(left_of(jnp.where(mask, gram, 0.0)), right) for gram, right in zip(grams, rights)
                ]
                inverses = [inv - mm(inv, middle) for inv, middle in zip(inverses, middles)]
            size *= 2
        vs = [mm(inv, w) for inv, w in zip(inverses, ws)]
        for i in range(count):
            v_buf[start + i] = vs[i]
            at_end(i, eye - mm(vs[i].T, ws[i]))

    first = []
    for i in range(half):
        first.append(remote(outgoing.at[i], pair.at[x, i], s_sem.at[0, i], r_sem.at[0, i], {"seq": partner}))

    def send_off(i, value):
        outgoing[i] = value
        first[i].start()

    def keep(i, value):
        pair[x, i] = value

    def done(i, value):
        @pl.when((i // half) == x)
        def _():
            pair[x, i % half] = value
        @pl.when((i // half) != x)
        def _():
            outgoing[i % half] = value
            first[i % half].start()
    group(0, heads, done)

    q_load.wait()
    k_load.wait()
    below = lax.broadcasted_iota(jnp.int32, (2 * tok, tok), 0) % tok >= lax.broadcasted_iota(jnp.int32, (2 * tok, tok), 1)
    for hh in range(heads):
        columns = slice(hh * dim, (hh + 1) * dim)
        targets = x_ref[:, columns]
        along = product_t(targets, jnp.concatenate(split(w_dir[hh]), axis=0))
        local[hh] = left_of(targets.astype(F32) - mm(jnp.where(below, along, 0.0), v_buf[hh]))

    rows = tok // CUTS
    pieces = [(i, pl.ds(r * rows, rows)) for i in range(half) for r in range(CUTS)]
    chained, last = [], []
    for p, (i, cut) in enumerate(pieces):
        chained.append(remote(ct.at[i, cut], chain.at[i, cut], s_sem.at[1, p], r_sem.at[1, p], {"seq": seq + 2}))
        last.append(remote(toward.at[i, cut], other.at[i, cut], s_sem.at[2, p], r_sem.at[2, p], {"seq": partner}))

    @pl.when(z == 0)
    def _():
        for i in range(half):
            chain[i] = eye

    for i in range(half):
        remote(outgoing.at[i], pair.at[1 - x, i], s_sem.at[0, i], r_sem.at[0, i], {"seq": partner}).wait_recv()
        even = right_of(pair[0, i])
        step = jnp.concatenate([right_of(product(left_of(pair[0, i]), right_of(pair[1, i]))), even], axis=1)
        for r in range(CUTS):
            p = i * CUTS + r
            cut = pieces[p][1]

            @pl.when(z > 0)
            def _():
                chained[p].wait_recv()

            before = chain[i, cut]
            after = jnp.dot(left_of(before), step, preferred_element_type=F32)
            ct[i, cut] = fold(after[:, :2 * dim])

            @pl.when(z < n_pairs - 1)
            def _():
                chained[p].start()

            odd = fold(after[:, 2 * dim:])
            toward[i, cut] = jnp.where(x == 0, odd, before)
            last[p].start()
            mine[i, cut] = jnp.where(x == 0, before, odd)

    for i in range(half):
        finish(x * half + i, mine[i], local, out_ref)
    for i in range(half):
        for r in range(CUTS):
            last[i * CUTS + r].wait_recv()
        finish((1 - x) * half + i, other[i], local, out_ref)

    to_near.wait_send()
    for c in range(CHUNKS):
        to_far[c].wait_send()
        to_across[c].wait_send()
    for i in range(half):
        first[i].wait_send()
    for copy in last:
        copy.wait_send()

    @pl.when(z < n_pairs - 1)
    def _():
        for copy in chained:
            copy.wait_send()


def finish(hh, entering, local, out_ref):
    hi, lo = split(entering)
    both = jnp.concatenate([jnp.concatenate([hi, hi], axis=1), jnp.concatenate([lo, lo], axis=1)], axis=0)
    out = product_t(local[hh], both).astype(BF16)
    columns = pl.ds(pl.multiple_of(hh * HEAD_DIM, HEAD_DIM), HEAD_DIM)
    out_ref[:, columns] = out


def part(both_ref, q_ref, k_ref):
    tok = q_ref.shape[0]
    q_ref[...] = both_ref[:tok]
    k_ref[...] = both_ref[tok:]


def solution(mesh):
    n_seq = mesh.shape["seq"]

    def body(features, proj_weight, query_vectors, key_vectors):
        tok, depth = features.shape
        width = proj_weight.shape[1]
        heads = width // HEAD_DIM
        half = heads // 2
        square = (HEAD_DIM, HEAD_DIM)
        vmem = pl.BlockSpec(memory_space=pltpu.VMEM)
        out = jax.ShapeDtypeStruct((tok, width), BF16)
        both = pl.pallas_call(
            functools.partial(kernel, n_seq),
            out_shape=jax.ShapeDtypeStruct((2 * tok, width), BF16),
            in_specs=[pl.BlockSpec(memory_space=pl.ANY)] * 4,
            out_specs=vmem,
            scratch_shapes=[
                pltpu.VMEM((tok, depth), BF16),
                pltpu.VMEM((2 * tok, width), BF16),
                pltpu.VMEM((4, depth, width), BF16),
                pltpu.VMEM((tok, depth), BF16),
                pltpu.VMEM((CHUNKS, tok, depth // CHUNKS), BF16),
                pltpu.VMEM((CHUNKS, tok, depth // CHUNKS), BF16),
                pltpu.VMEM((heads, tok, HEAD_DIM), F32),
                pltpu.VMEM((heads, tok, HEAD_DIM), F32),
                pltpu.VMEM((heads, tok, HEAD_DIM), F32),
                pltpu.VMEM((heads, 2 * tok, 2 * HEAD_DIM), BF16),
                pltpu.VMEM((2, half) + square, F32),
                pltpu.VMEM((half,) + square, F32),
                pltpu.VMEM((half,) + square, F32),
                pltpu.VMEM((half,) + square, F32),
                pltpu.VMEM((half,) + square, F32),
                pltpu.VMEM((half,) + square, F32),
                pltpu.VMEM((half,) + square, F32),
                pltpu.SemaphoreType.DMA((7,)),
                pltpu.SemaphoreType.DMA((1 + 2 * CHUNKS,)),
                pltpu.SemaphoreType.DMA((1 + 2 * CHUNKS,)),
                pltpu.SemaphoreType.DMA((3, half * CUTS)),
                pltpu.SemaphoreType.DMA((3, half * CUTS)),
            ],
            compiler_params=pltpu.CompilerParams(
                collective_id=0, has_side_effects=True, vmem_limit_bytes=56 * 1024 * 1024
            ),
            cost_estimate=pl.CostEstimate(flops=4_000_000_000, bytes_accessed=10_000_000, transcendentals=0),
        )(features, proj_weight, query_vectors, key_vectors)
        return pl.pallas_call(part, out_shape=(out, out), in_specs=[vmem], out_specs=(vmem, vmem))(both)

    in_specs = (P("seq", "head"), P(None, "head"), P("seq", "head"), P("seq", "head"))
    out_specs = (P("seq", "head"), P("seq", "head"))
    return jax.shard_map(body, mesh=mesh, in_specs=in_specs, out_specs=out_specs, check_vma=False)
```
